32 devices in a mesh: section: 2 (over y), grp: 4 (over x, core), tok: 4 (over z).
Axes of the slice: x: 2, y: 2, z: 4, core: 2. Of those that a mesh axis runs over, the one named last changes fastest.
Arguments:
- image_in: bfloat16 [2, 4, 128, 3072], P('section', 'grp', 'tok'), may hold values from -1.5 to 1.5
- text_in: bfloat16 [2, 4, 512, 3072], P('section', 'grp', 'tok'), may hold values from -1.5 to 1.5
- text_length: int32 [4], P('grp'), may hold values from 256 to 512, as said below
- entry_order: int32 [4, 4], P('grp'), may hold values from 0 to 3, as said below
- step_index: int32 [4, 4], P('grp'), may hold values from 0 to 3
- image_modulation: bfloat16 [2, 4, 18432], P('section'), may hold values from -3 to 3
- text_modulation: bfloat16 [2, 4, 9216], P('section'), may hold values from -3 to 3
- image_to_heads: bfloat16 [2, 3072, 9216], P('section', None, 'tok'), may hold values from -0.109375 to 0.109375
- text_to_heads: bfloat16 [2, 3072, 9216], P('section', None, 'tok'), may hold values from -0.109375 to 0.109375
- head_gain: float32 [2, 4, 128], P('section'), may hold values from 0.5 to 2
- image_from_heads: bfloat16 [2, 3072, 3072], P('section', None, 'tok'), may hold values from -0.109375 to 0.109375
- text_from_heads: bfloat16 [2, 3072, 3072], P('section', None, 'tok'), may hold values from -0.109375 to 0.109375
- image_up: bfloat16 [2, 3072, 12288], P('section', None, 'tok'), may hold values from -0.109375 to 0.109375
- image_down: bfloat16 [2, 12288, 3072], P('section', 'tok'), may hold values from -0.0546875 to 0.0546875
- stale_cache: bfloat16 [2, 4, 512, 6144], P('section', 'grp', 'tok'), may hold values from -400 to 400
- final_modulation: bfloat16 [4, 6144], replicated, may hold values from -3 to 3
- final_weight: bfloat16 [3072, 64], P(None, 'section'), may hold values from -0.109375 to 0.109375
- latents: float32 [4, 128, 64], P('grp', 'tok', 'section'), may hold values from -6 to 6
Outputs:
- image_handoff: bfloat16 [2, 4, 128, 3072], P('section', 'grp', 'tok')
- text_handoff: bfloat16 [2, 4, 512, 3072], P('section', 'grp', 'tok')
- fresh_cache: bfloat16 [2, 4, 512, 6144], P('section', 'grp', 'tok')
- latents_next: float32 [4, 128, 64], P('grp', 'tok', 'section')
The draws below stay inside these ranges and needn't reach their ends.
Inputs may be any that keep to these rules, and one draw needn't show every extreme that they name: `text_length`: valid text tokens of each request; some request has exactly 512. `entry_order`: each row is a permutation of the 4 patch numbers.
All inputs are finite; a program needn't handle non-finite values.
Results may differ from the reference program's by a relative error of at most 0.023.
The reference program's roundings to bfloat16 on the way (of `attended`, `text_out`, `hidden` and `image_out`) count: a program that leaves them out, or rounds other values in their place, can miss the bound.
Values may be sent and summed in bfloat16 or wider, within the bound.
A program may use at most 192 MiB of HBM per device.

```python
import jax
import jax.numpy as jnp
from jax import lax

D = 3072
HEADS = 24
HDIM = 128
FF = 12288
CH = 64
IMG = 512
TXT = 512
PATCHES = 4
TSTEPS = 4
LAYERS = 2
REQUESTS = 4
PATCH = 128


def draw_text_length(key, part):
    lengths = jax.random.randint(key, (REQUESTS,), TXT // 2, TXT + 1)
    chosen = jax.random.randint(jax.random.fold_in(key, 1), (), 0, REQUESTS)
    return jnp.where(jnp.arange(REQUESTS) == chosen, TXT, lengths).astype(jnp.int32)


def draw_entry_order(key, part):
    scores = jax.random.randint(jax.random.fold_in(key, 23), (REQUESTS, PATCHES), 0, 1 << 20)
    scores = scores * PATCHES + jnp.arange(PATCHES, dtype=jnp.int32)[None, :]
    return jnp.argsort(scores, axis=1, stable=True).astype(jnp.int32)


def draw_stale_cache(key, part):
    shape = (LAYERS, REQUESTS, IMG, 2 * D)
    values = jax.random.normal(key, shape, jnp.float32)
    values = jnp.clip(values, -400.0, 400.0)
    return values.astype(jnp.bfloat16)


def plant(entries, key, low, largest):
    longest = entries.shape.index(max(entries.shape))
    spots = []
    for shift in (0, 1):
        where = [jax.random.randint(jax.random.fold_in(key, axis), (), 0, length) for axis, length in enumerate(entries.shape)]
        where[longest] = (where[longest] + shift) % entries.shape[longest]
        spots.append(tuple(where))
    return entries.at[spots[0]].set(low).at[spots[1]].set(largest)


def block_scale(rng, extent, cuts, least, high):
    factor_of, own = 1.0, jax.random.fold_in(rng, 6)
    for position, shards_of in cuts:
        steps = jnp.exp(jax.random.uniform(jax.random.fold_in(own, position), (shards_of,), jnp.float32, least / len(cuts), high / len(cuts)))
        factor_of = factor_of * jnp.repeat(steps, extent[position] // shards_of).reshape([-1 if axis == position else 1 for axis in range(len(extent))])
    return factor_of


def scatter_about(rng, shape, scale, bound, shards=(), kind=jnp.bfloat16):
    factor_of = block_scale(rng, shape, shards, -0.22, 0.18) if shards else 1.0
    array = jax.random.normal(rng, shape, jnp.float32) * scale * factor_of
    return jnp.minimum(jnp.maximum(array, -bound), bound).astype(kind)


def setup_inputs(seed: int = 0) -> dict:
    key_of = jax.random.split(jax.random.key(seed), 19)
    image_in = scatter_about(key_of[0], (LAYERS, REQUESTS, PATCH, D), 0.25, 1.5, ((0, 2), (1, 4), (2, 4)))
    text_in = scatter_about(key_of[1], (LAYERS, REQUESTS, TXT, D), 0.25, 1.5, ((0, 2), (1, 4), (2, 4)))
    text_length = draw_text_length(jax.random.fold_in(key_of[18], 71), 0)
    entry_order = draw_entry_order(jax.random.fold_in(key_of[18], 71), 0)
    step_index = plant(jax.random.randint(key_of[4], (REQUESTS, PATCHES), 0, TSTEPS), jax.random.fold_in(key_of[4], 1), 0, TSTEPS - 1).astype(jnp.int32)
    image_modulation = scatter_about(key_of[5], (LAYERS, TSTEPS, 6 * D), 0.5, 3.0, ((0, 2),))
    text_modulation = scatter_about(key_of[6], (LAYERS, TSTEPS, 3 * D), 0.5, 3.0, ((0, 2),))
    image_to_heads = scatter_about(key_of[7], (LAYERS, D, 3 * D), D ** -0.5, 0.109375, ((0, 2), (2, 4)))
    text_to_heads = scatter_about(key_of[8], (LAYERS, D, 3 * D), D ** -0.5, 0.109375, ((0, 2), (2, 4)))
    head_gain = jnp.clip(0.5 + 1.5 * jax.random.uniform(key_of[9], (LAYERS, 4, HDIM), jnp.float32) ** block_scale(key_of[9], (LAYERS, 4, HDIM), ((0, 2),), -0.2, 0.2), 0.5, 2.0)
    image_from_heads = scatter_about(key_of[10], (LAYERS, D, D), D ** -0.5, 0.109375, ((0, 2), (2, 4)))
    text_from_heads = scatter_about(key_of[11], (LAYERS, D, D), D ** -0.5, 0.109375, ((0, 2), (2, 4)))
    image_up = scatter_about(key_of[12], (LAYERS, D, FF), D ** -0.5, 0.109375, ((0, 2), (2, 4)))
    image_down = scatter_about(key_of[13], (LAYERS, FF, D), FF ** -0.5, 0.0546875, ((0, 2), (1, 4)))
    stale_cache = draw_stale_cache(jax.random.fold_in(key_of[18], 71), 0)
    final_modulation = scatter_about(key_of[15], (TSTEPS, 2 * D), 0.5, 3.0)
    final_weight = scatter_about(key_of[16], (D, CH), D ** -0.5, 0.109375, ((1, 2),))
    latents = scatter_about(key_of[17], (REQUESTS, PATCH, CH), 1.0, 6.0, ((0, 4), (1, 4), (2, 2)), jnp.float32)
    return {"image_in": image_in, "text_in": text_in, "text_length": text_length, "entry_order": entry_order, "step_index": step_index, "image_modulation": image_modulation, "text_modulation": text_modulation, "image_to_heads": image_to_heads, "text_to_heads": text_to_heads, "head_gain": head_gain, "image_from_heads": image_from_heads, "text_from_heads": text_from_heads, "image_up": image_up, "image_down": image_down, "stale_cache": stale_cache, "final_modulation": final_modulation, "final_weight": final_weight, "latents": latents}


eps = 1e-06

def stored(field):
    return lax.optimization_barrier(field.astype(jnp.bfloat16))

def layer_norm(field):
    mean = lax.optimization_barrier(jnp.mean(field, axis=-1, keepdims=True))
    centred = field - mean
    spread = lax.optimization_barrier(jnp.mean(centred * centred, axis=-1, keepdims=True))
    return centred * lax.rsqrt(spread + eps)

def modulate(field, shift, scale):
    return layer_norm(field) * (1.0 + scale) + shift

def head_norm(field, gain):
    height = field.shape[0]
    shaped = field.reshape(height, HEADS, HDIM)
    power = lax.optimization_barrier(jnp.mean(shaped * shaped, axis=-1, keepdims=True))
    return (shaped * lax.rsqrt(power + eps) * gain).reshape(height, HEADS * HDIM)

def attention(queries, keys, values, valid):
    height = queries.shape[0]
    query_f = queries.astype(jnp.float32).reshape(height, HEADS, HDIM)
    key_f = keys.astype(jnp.float32).reshape(keys.shape[0], HEADS, HDIM)
    value_f = values.astype(jnp.float32).reshape(values.shape[0], HEADS, HDIM)
    scores = jnp.einsum('qhd,khd->qhk', query_f, key_f) * HDIM ** (-0.5)
    scores = jnp.where(valid[None, None, :], scores, -1e+30)
    highest = lax.optimization_barrier(jnp.max(scores, axis=-1, keepdims=True))
    expo = jnp.where(valid[None, None, :], jnp.exp(scores - highest), 0.0)
    total = lax.optimization_barrier(jnp.sum(expo, axis=-1))
    weights = stored(expo).astype(jnp.float32)
    mixed = jnp.einsum('qhk,khd->qhd', weights, value_f) / total[..., None]
    return mixed.reshape(height, HEADS * HDIM).astype(jnp.bfloat16)

def reference(image_in, text_in, text_length, entry_order, step_index, image_modulation, text_modulation, image_to_heads, text_to_heads, head_gain, image_from_heads, text_from_heads, image_up, image_down, stale_cache, final_modulation, final_weight, latents):
    image_layers = []
    text_layers = []
    cache_layers = []
    for layer in range(LAYERS):
        image_reqs = []
        text_reqs = []
        cache_reqs = []
        for request in range(REQUESTS):
            patch = entry_order[request, layer]
            step_now = step_index[request, patch]
            modul = lax.dynamic_index_in_dim(image_modulation[layer], step_now, 0, False).astype(jnp.float32).reshape(6, D)
            text_mod = lax.dynamic_index_in_dim(text_modulation[layer], step_now, 0, False).astype(jnp.float32).reshape(3, D)
            image_x = image_in[layer, request].astype(jnp.float32)
            text_x = text_in[layer, request].astype(jnp.float32)
            image_normed = modulate(image_x, modul[0], modul[1]).astype(jnp.bfloat16)
            text_normed = modulate(text_x, text_mod[0], text_mod[1]).astype(jnp.bfloat16)
            image_proj = stored(jnp.dot(image_normed, image_to_heads[layer], preferred_element_type=jnp.float32))
            text_proj = stored(jnp.dot(text_normed, text_to_heads[layer], preferred_element_type=jnp.float32))
            gains = head_gain[layer]
            image_query = head_norm(image_proj[:, :D].astype(jnp.float32), gains[0]).astype(jnp.bfloat16)
            image_key = head_norm(image_proj[:, D:2 * D].astype(jnp.float32), gains[1]).astype(jnp.bfloat16)
            text_query = head_norm(text_proj[:, :D].astype(jnp.float32), gains[2]).astype(jnp.bfloat16)
            text_key = head_norm(text_proj[:, D:2 * D].astype(jnp.float32), gains[3]).astype(jnp.bfloat16)
            fresh = jnp.concatenate([image_key, image_proj[:, 2 * D:]], axis=1)
            begin = (patch * PATCH).astype(jnp.int32)
            cache = lax.dynamic_update_slice(stale_cache[layer, request], fresh, (begin, jnp.zeros((), jnp.int32)))
            keys = jnp.concatenate([text_key, cache[:, :D]], axis=0)
            values = jnp.concatenate([text_proj[:, 2 * D:], cache[:, D:]], axis=0)
            valid = jnp.concatenate([jnp.arange(TXT, dtype=jnp.int32) < text_length[request], jnp.ones((IMG,), bool)])
            queries = jnp.concatenate([image_query, text_query], axis=0)
            attended = attention(queries, keys, values, valid)
            image_back = stored(jnp.dot(attended[:PATCH], image_from_heads[layer], preferred_element_type=jnp.float32))
            text_back = stored(jnp.dot(attended[PATCH:], text_from_heads[layer], preferred_element_type=jnp.float32))
            image_mid = image_x + modul[2] * image_back.astype(jnp.float32)
            text_out = (text_x + text_mod[2] * text_back.astype(jnp.float32)).astype(jnp.bfloat16)
            mlp_normed = modulate(image_mid, modul[3], modul[4]).astype(jnp.bfloat16)
            hidden = jax.nn.gelu(jnp.dot(mlp_normed, image_up[layer], preferred_element_type=jnp.float32), approximate=True).astype(jnp.bfloat16)
            reduced = jnp.dot(hidden, image_down[layer], preferred_element_type=jnp.float32)
            image_out = (image_mid + modul[5] * reduced).astype(jnp.bfloat16)
            image_reqs.append(image_out)
            text_reqs.append(text_out)
            cache_reqs.append(cache)
        image_layers.append(jnp.stack(image_reqs))
        text_layers.append(jnp.stack(text_reqs))
        cache_layers.append(jnp.stack(cache_reqs))
    image_stack = jnp.stack(image_layers)
    text_stack = jnp.stack(text_layers)
    fresh_cache = jnp.stack(cache_layers)
    image_handoff = jnp.roll(image_stack, 1, axis=0)
    text_handoff = jnp.roll(text_stack, 1, axis=0)
    updated = []
    for request in range(REQUESTS):
        patch_last = entry_order[request, LAYERS - 1]
        step_last = step_index[request, patch_last]
        final_mod = lax.dynamic_index_in_dim(final_modulation, step_last, 0, False).astype(jnp.float32).reshape(2, D)
        source = image_stack[LAYERS - 1, request].astype(jnp.float32)
        normed = modulate(source, final_mod[0], final_mod[1]).astype(jnp.bfloat16)
        velocity = jnp.dot(normed, final_weight, preferred_element_type=jnp.float32)
        updated.append(latents[request] + -1.0 / TSTEPS * velocity)
    latents_next = jnp.stack(updated)
    return (image_handoff, text_handoff, fresh_cache, latents_next)
```

```python
import jax
import jax.numpy as jnp
from jax import lax
from jax.experimental import pallas as pl
from jax.experimental.pallas import tpu as pltpu
from jax.sharding import PartitionSpec as P

HDIM = 128
TSTEPS = 4
PATCHES = 4


eps = 1e-06
masked_score = -1e30


def from_behind(block, axis, distance):
    devices = range(lax.axis_size(axis))
    route = [((i - distance) % len(devices), i) for i in devices]
    return lax.ppermute(block, axis, route)


def layer_norm(field):
    mean = jnp.mean(field, axis=-1, keepdims=True)
    centred = field - mean
    spread = jnp.mean(centred * centred, axis=-1, keepdims=True)
    return centred * lax.rsqrt(spread + eps)


def modulate(field, shift, scale):
    return layer_norm(field) * (1.0 + scale) + shift


def head_norm(field, gain):
    height, width = field.shape
    shaped = field.reshape(height, width // HDIM, HDIM)
    power = jnp.mean(shaped * shaped, axis=-1, keepdims=True)
    return (shaped * lax.rsqrt(power + eps) * gain).reshape(height, width)


def attend(carry, queries, piece, valid):
    highest, total, mixed = carry
    height, width = queries.shape
    heads = width // HDIM
    keys = piece[:, :width].reshape(-1, heads, HDIM)
    values = piece[:, width:].reshape(-1, heads, HDIM)
    scores = jnp.einsum(
        "qhd,khd->qhk",
        queries.reshape(height, heads, HDIM),
        keys,
        preferred_element_type=jnp.float32,
    ) * HDIM ** (-0.5)
    scores = jnp.where(valid[None, None, :], scores, masked_score)
    new_high = jnp.maximum(highest, jnp.max(scores, axis=-1))
    expo = jnp.where(valid[None, None, :], jnp.exp(scores - new_high[..., None]), 0.0)
    keep = jnp.exp(highest - new_high)
    total = total * keep + jnp.sum(expo, axis=-1)
    mixed = mixed * keep[..., None] + jnp.einsum(
        "qhk,khd->qhd", expo.astype(jnp.bfloat16), values, preferred_element_type=jnp.float32
    )
    return (new_high, total, mixed)


def empty_carry(height, heads):
    return (
        jnp.full((height, heads), masked_score, jnp.float32),
        jnp.zeros((height, heads), jnp.float32),
        jnp.zeros((height, heads, HDIM), jnp.float32),
    )


def shards(
    image_in,
    text_in,
    text_length,
    entry_order,
    step_index,
    image_modulation,
    text_modulation,
    image_to_heads,
    text_to_heads,
    head_gain,
    image_from_heads,
    text_from_heads,
    image_up,
    image_down,
    stale_cache,
    final_modulation,
    final_weight,
    latents,
):
    section = lax.axis_index("section")
    last_section = lax.axis_size("section") - 1
    position = lax.axis_index("tok")
    image_x = image_in[0, 0].astype(jnp.float32)
    text_x = text_in[0, 0].astype(jnp.float32)
    image_rows = image_x.shape[0]
    width = image_x.shape[1]
    heads = width // HDIM
    patch = lax.dynamic_index_in_dim(entry_order[0], section, 0, False)
    step_now = lax.dynamic_index_in_dim(step_index[0], patch, 0, False)
    modul = (
        lax.dynamic_index_in_dim(image_modulation[0], step_now, 0, False)
        .astype(jnp.float32)
        .reshape(6, width)
    )
    text_mod = (
        lax.dynamic_index_in_dim(text_modulation[0], step_now, 0, False)
        .astype(jnp.float32)
        .reshape(3, width)
    )
    image_normed = modulate(image_x, modul[0], modul[1]).astype(jnp.bfloat16)
    text_normed = modulate(text_x, text_mod[0], text_mod[1]).astype(jnp.bfloat16)
    every_image, every_text = (
        lax.all_gather(image_normed, "tok", axis=0, tiled=True),
        lax.all_gather(text_normed, "tok", axis=0, tiled=True),
    )
    image_cols = jnp.dot(every_image, image_to_heads[0], preferred_element_type=jnp.float32).astype(
        jnp.bfloat16
    )
    text_cols = jnp.dot(every_text, text_to_heads[0], preferred_element_type=jnp.float32).astype(
        jnp.bfloat16
    )
    image_proj, text_proj = (
        lax.all_to_all(image_cols, "tok", split_axis=0, concat_axis=1, tiled=True),
        lax.all_to_all(text_cols, "tok", split_axis=0, concat_axis=1, tiled=True),
    )
    gains = head_gain[0]
    image_query = head_norm(image_proj[:, :width].astype(jnp.float32), gains[0]).astype(
        jnp.bfloat16
    )
    image_key = head_norm(image_proj[:, width : 2 * width].astype(jnp.float32), gains[1]).astype(
        jnp.bfloat16
    )
    text_query = head_norm(text_proj[:, :width].astype(jnp.float32), gains[2]).astype(jnp.bfloat16)
    text_key = head_norm(text_proj[:, width : 2 * width].astype(jnp.float32), gains[3]).astype(
        jnp.bfloat16
    )
    fresh_image = jnp.concatenate([image_key, image_proj[:, 2 * width :]], axis=1)
    fresh_text = jnp.concatenate([text_key, text_proj[:, 2 * width :]], axis=1)
    queries = jnp.concatenate([image_query, text_query], axis=0)
    query_rows = queries.shape[0]
    patch_rows = lax.all_gather(fresh_image, "tok", axis=0, tiled=True)
    stale = stale_cache[0, 0]
    cache_rows = stale.shape[0]
    patch_len = patch_rows.shape[0]
    first_row = position * cache_rows
    begin = patch * patch_len
    offset = jnp.clip(first_row - begin, 0, patch_len - cache_rows)
    window = lax.dynamic_slice_in_dim(patch_rows, offset, cache_rows, 0)
    inside = jnp.logical_and(first_row >= begin, first_row < begin + patch_len)
    current = jnp.where(inside, window, stale)
    text_count = text_length[0]
    piece = lax.all_gather(current, "tok", axis=0, tiled=True)
    carry = attend(
        empty_carry(query_rows, heads), queries, piece, jnp.ones((piece.shape[0],), bool)
    )
    piece = lax.all_gather(fresh_text, "tok", axis=0, tiled=True)
    where_text = jnp.arange(piece.shape[0], dtype=jnp.int32)
    highest, total, mixed = attend(carry, queries, piece, where_text < text_count)
    attended = (mixed / total[..., None]).reshape(query_rows, width).astype(jnp.bfloat16)
    every_image_att, every_text_att = (
        lax.all_gather(attended[:image_rows], "tok", axis=0, tiled=True),
        lax.all_gather(attended[image_rows:], "tok", axis=0, tiled=True),
    )
    image_back_cols = jnp.dot(
        every_image_att, image_from_heads[0], preferred_element_type=jnp.float32
    ).astype(jnp.bfloat16)
    text_back_cols = jnp.dot(
        every_text_att, text_from_heads[0], preferred_element_type=jnp.float32
    ).astype(jnp.bfloat16)
    image_back, text_back = (
        lax.all_to_all(image_back_cols, "tok", split_axis=0, concat_axis=1, tiled=True),
        lax.all_to_all(text_back_cols, "tok", split_axis=0, concat_axis=1, tiled=True),
    )
    image_mid = image_x + modul[2] * image_back.astype(jnp.float32)
    text_out = (text_x + text_mod[2] * text_back.astype(jnp.float32)).astype(jnp.bfloat16)
    mlp_normed = modulate(image_mid, modul[3], modul[4]).astype(jnp.bfloat16)
    up_weight = image_up[0]
    down_weight = image_down[0]
    hidden = jax.nn.gelu(
        jnp.dot(
            lax.all_gather(mlp_normed, "tok", axis=0, tiled=True),
            up_weight,
            preferred_element_type=jnp.float32,
        ),
        approximate=True,
    ).astype(jnp.bfloat16)
    reduced = lax.psum_scatter(
        jnp.dot(hidden, down_weight, preferred_element_type=jnp.float32),
        "tok",
        scatter_dimension=0,
        tiled=True,
    )
    image_out = (image_mid + modul[5] * reduced).astype(jnp.bfloat16)
    joined = from_behind(jnp.concatenate([image_out, text_out], axis=0), "section", 1)
    image_next = joined[:image_rows]
    text_next = joined[image_rows:]
    final_source = jnp.where(section == last_section, image_out, image_next)
    patch_last = entry_order[0, last_section]
    step_last = lax.dynamic_index_in_dim(step_index[0], patch_last, 0, False)
    final_mod = (
        lax.dynamic_index_in_dim(final_modulation, step_last, 0, False)
        .astype(jnp.float32)
        .reshape(2, width)
    )
    normed = modulate(final_source.astype(jnp.float32), final_mod[0], final_mod[1]).astype(
        jnp.bfloat16
    )
    velocity = jnp.dot(normed, final_weight, preferred_element_type=jnp.float32)
    latents_next = latents[0] + -1.0 / TSTEPS * velocity
    return (image_next[None, None], text_next[None, None], current[None, None], latents_next[None])


def unit_rms(block, gain):
    power = jnp.mean(block * block, axis=-1, keepdims=True)
    return (block * lax.rsqrt(power + eps) * gain).astype(jnp.bfloat16)


def head_kernel(
    patch_ref, count_ref, q_ref, k_ref, v_ref, ks_ref, vs_ref, gain_ref, out_ref, keys, values
):
    cache_rows = ks_ref.shape[0]
    rows = k_ref.shape[0]
    image_rows = rows - (keys.shape[0] - cache_rows)
    text_rows = rows - image_rows
    gains = gain_ref[...]
    f32 = jnp.float32
    begin = pl.multiple_of(patch_ref[0] * image_rows, image_rows)
    keys[pl.ds(0, cache_rows), :] = ks_ref[...]
    values[pl.ds(0, cache_rows), :] = vs_ref[...]
    keys[pl.ds(begin, image_rows), :] = unit_rms(k_ref[pl.ds(0, image_rows), :].astype(f32), gains[1:2])
    values[pl.ds(begin, image_rows), :] = v_ref[pl.ds(0, image_rows), :]
    keys[pl.ds(cache_rows, text_rows), :] = unit_rms(
        k_ref[pl.ds(image_rows, text_rows), :].astype(f32), gains[3:4]
    )
    values[pl.ds(cache_rows, text_rows), :] = v_ref[pl.ds(image_rows, text_rows), :]
    all_keys = keys[...]
    all_values = values[...]
    column = lax.broadcasted_iota(jnp.int32, (1, cache_rows + text_rows), 1)
    valid = column < cache_rows + count_ref[0]
    chunk = image_rows
    for part in range(rows // chunk):
        span = pl.ds(part * chunk, chunk)
        gain = gains[0:1] if part == 0 else gains[2:3]
        query = unit_rms(q_ref[span, :].astype(f32), gain)
        scores = lax.dot_general(
            query, all_keys, (((1,), (1,)), ((), ())), preferred_element_type=f32
        ) * HDIM ** (-0.5)
        scores = jnp.where(valid, scores, masked_score)
        highest = jnp.max(scores, axis=-1, keepdims=True)
        expo = jnp.exp(scores - highest)
        total = jnp.sum(expo, axis=-1, keepdims=True)
        mixed = jnp.dot(expo.astype(jnp.bfloat16), all_values, preferred_element_type=f32)
        out_ref[span, :] = (mixed / total).astype(jnp.bfloat16)


def head_attention(patch, count, q, k, v, stale_k, stale_v, gains):
    rows, width = q.shape
    cache_rows = stale_k.shape[0]
    image_rows = patch_rows_of(cache_rows)
    total_keys = cache_rows + rows - image_rows
    tall = pl.BlockSpec((rows, HDIM), lambda h, *_: (0, h))
    kept = pl.BlockSpec((cache_rows, HDIM), lambda h, *_: (0, h))
    return pl.pallas_call(
        head_kernel,
        out_shape=jax.ShapeDtypeStruct((rows, width), jnp.bfloat16),
        grid_spec=pltpu.PrefetchScalarGridSpec(
            num_scalar_prefetch=2,
            grid=(width // HDIM,),
            in_specs=[
                tall,
                tall,
                tall,
                kept,
                kept,
                pl.BlockSpec((4, HDIM), lambda h, *_: (0, 0)),
            ],
            out_specs=tall,
            scratch_shapes=[
                pltpu.VMEM((total_keys, HDIM), jnp.bfloat16),
                pltpu.VMEM((total_keys, HDIM), jnp.bfloat16),
            ],
        ),
        compiler_params=pltpu.CompilerParams(vmem_limit_bytes=32 * 1024 * 1024),
        cost_estimate=pl.CostEstimate(
            flops=4 * rows * total_keys * width,
            bytes_accessed=2 * width * (4 * rows + 2 * cache_rows),
            transcendentals=rows * total_keys * (width // HDIM),
        ),
    )(patch[None], count[None], q, k, v, stale_k, stale_v, gains)


def patch_rows_of(cache_rows):
    return cache_rows // PATCHES


def swap_heads(cols, position):
    count = lax.axis_size("tok")
    block = cols.shape[1] // 3
    first, second, third = (cols[:, i * block : (i + 1) * block] for i in range(3))
    even = position % 2 == 0
    near = lax.ppermute(second, "tok", [(0, 1), (1, 0), (2, 3), (3, 2)])
    far = lax.ppermute(
        jnp.where(even, third, first), "tok", [(0, 2), (2, 0), (1, 3), (3, 1)]
    )
    stay = jnp.where(even, first, third)
    query = jnp.where(position == 0, stay, jnp.where(position == 1, near, far))
    key = jnp.where((position == 0) | (position == 3), near, stay)
    value = jnp.where(position == 3, stay, jnp.where(position == 2, near, far))
    return query, key, value


def shards_by_head(
    image_in,
    text_in,
    text_length,
    entry_order,
    step_index,
    image_modulation,
    text_modulation,
    image_to_heads,
    text_to_heads,
    head_gain,
    image_from_heads,
    text_from_heads,
    image_up,
    image_down,
    stale_cache,
    final_modulation,
    final_weight,
    latents,
):
    f32, bf16 = jnp.float32, jnp.bfloat16
    section = lax.axis_index("section")
    last_section = lax.axis_size("section") - 1
    position = lax.axis_index("tok")
    count = lax.axis_size("tok")
    text_x = text_in[0, 0].astype(f32)
    image_rows, width = image_in.shape[2:]
    text_rows = text_in.shape[2]
    patch_len = image_rows * count
    share = width // count
    patch = lax.dynamic_index_in_dim(entry_order[0], section, 0, False)
    step_now = lax.dynamic_index_in_dim(step_index[0], patch, 0, False)
    modul = (
        lax.dynamic_index_in_dim(image_modulation[0], step_now, 0, False)
        .astype(f32)
        .reshape(6, width)
    )
    text_mod = (
        lax.dynamic_index_in_dim(text_modulation[0], step_now, 0, False)
        .astype(f32)
        .reshape(3, width)
    )
    stale = stale_cache[0, 0]
    cache_rows = stale.shape[0]
    stale_heads = lax.all_to_all(
        stale.reshape(cache_rows, 2, count, share), "tok", split_axis=2, concat_axis=0, tiled=False
    )
    stale_k = stale_heads[:, :, 0].reshape(count * cache_rows, share)
    stale_v = stale_heads[:, :, 1].reshape(count * cache_rows, share)
    text_normed = modulate(text_x, text_mod[0], text_mod[1]).astype(bf16)
    own = jnp.concatenate([image_in[0, 0], text_normed], axis=0)
    every = lax.all_gather(own, "tok", axis=0, tiled=False)
    every_image_x = every[:, :image_rows].reshape(patch_len, width).astype(f32)
    every_text = every[:, image_rows:].reshape(count * text_rows, width)
    every_image = modulate(every_image_x, modul[0], modul[1]).astype(bf16)
    image_cols = jnp.dot(every_image, image_to_heads[0], preferred_element_type=f32).astype(bf16)
    text_cols = jnp.dot(every_text, text_to_heads[0], preferred_element_type=f32).astype(bf16)
    query, key, value = swap_heads(jnp.concatenate([image_cols, text_cols], axis=0), position)
    gains = head_gain[0]
    image_key = head_norm(key[:patch_len].astype(f32), gains[1]).astype(bf16)
    attended = head_attention(patch, text_length[0], query, key, value, stale_k, stale_v, gains)
    fresh = lax.all_gather(
        jnp.stack([image_key, value[:patch_len]], axis=0), "tok", axis=0, tiled=False
    )
    patch_rows = fresh.transpose(2, 1, 0, 3).reshape(patch_len, 2 * width)
    first_row = position * cache_rows
    begin = patch * patch_len
    offset = jnp.clip(first_row - begin, 0, patch_len - cache_rows)
    window = lax.dynamic_slice_in_dim(patch_rows, offset, cache_rows, 0)
    inside = jnp.logical_and(first_row >= begin, first_row < begin + patch_len)
    current = jnp.where(inside, window, stale)
    every_att = lax.all_gather(attended, "tok", axis=0, tiled=False)
    image_back_cols = jnp.einsum(
        "trd,tdc->rc",
        every_att[:, :patch_len],
        image_from_heads[0].reshape(count, share, share),
        preferred_element_type=f32,
    ).astype(bf16)
    text_back_cols = jnp.einsum(
        "trd,tdc->rc",
        every_att[:, patch_len:],
        text_from_heads[0].reshape(count, share, share),
        preferred_element_type=f32,
    ).astype(bf16)
    image_back = lax.all_gather(image_back_cols, "tok", axis=1, tiled=True)
    text_back = lax.all_to_all(text_back_cols, "tok", split_axis=0, concat_axis=1, tiled=True)
    image_mid = every_image_x + modul[2] * image_back.astype(f32)
    text_out = (text_x + text_mod[2] * text_back.astype(f32)).astype(bf16)
    text_next = from_behind(text_out, "section", 1)
    mlp_normed = modulate(image_mid, modul[3], modul[4]).astype(bf16)
    hidden = jax.nn.gelu(
        jnp.dot(mlp_normed, image_up[0], preferred_element_type=f32), approximate=True
    ).astype(bf16)
    partial = jnp.dot(hidden, image_down[0], preferred_element_type=f32)
    parts = lax.all_to_all(
        partial.astype(bf16).reshape(count, image_rows, width),
        "tok",
        split_axis=0,
        concat_axis=0,
        tiled=False,
    )
    reduced = jnp.sum(parts.astype(f32), axis=0)
    mid_own = lax.dynamic_slice_in_dim(image_mid, position * image_rows, image_rows, 0)
    image_out = (mid_own + modul[5] * reduced).astype(bf16)
    image_next = from_behind(image_out, "section", 1)
    final_source = jnp.where(section == last_section, image_out, image_next)
    patch_last = entry_order[0, last_section]
    step_last = lax.dynamic_index_in_dim(step_index[0], patch_last, 0, False)
    final_mod = (
        lax.dynamic_index_in_dim(final_modulation, step_last, 0, False)
        .astype(f32)
        .reshape(2, width)
    )
    normed = modulate(final_source.astype(f32), final_mod[0], final_mod[1]).astype(bf16)
    velocity = jnp.dot(normed, final_weight, preferred_element_type=f32)
    latents_next = latents[0] + -1.0 / TSTEPS * velocity
    return (image_next[None, None], text_next[None, None], current[None, None], latents_next[None])


def solution(mesh):
    placed = (
        P("section", "grp", "tok", None),
        P("section", "grp", "tok", None),
        P("grp"),
        P("grp", None),
        P("grp", None),
        P("section", None, None),
        P("section", None, None),
        P("section", None, "tok"),
        P("section", None, "tok"),
        P("section", None, None),
        P("section", None, "tok"),
        P("section", None, "tok"),
        P("section", None, "tok"),
        P("section", "tok", None),
        P("section", "grp", "tok", None),
        P(),
        P(None, "section"),
        P("grp", "tok", "section"),
    )
    return jax.shard_map(
        shards_by_head if mesh.shape["tok"] == 4 else shards,
        mesh=mesh,
        in_specs=placed,
        out_specs=(
            P("section", "grp", "tok", None),
            P("section", "grp", "tok", None),
            P("section", "grp", "tok", None),
            P("grp", "tok", "section"),
        ),
        check_vma=False,
    )
```

```python
import jax
import jax.numpy as jnp
from jax import lax
from jax.experimental import pallas as pl
from jax.experimental.pallas import tpu as pltpu
from jax.sharding import PartitionSpec as P

HDIM = 128
TSTEPS = 4
PATCHES = 4


eps = 1e-06
masked_score = -1e30


def from_behind(block, axis, distance):
    devices = range(lax.axis_size(axis))
    route = [((i - distance) % len(devices), i) for i in devices]
    return lax.ppermute(block, axis, route)


def layer_norm(field):
    mean = jnp.mean(field, axis=-1, keepdims=True)
    centred = field - mean
    spread = jnp.mean(centred * centred, axis=-1, keepdims=True)
    return centred * lax.rsqrt(spread + eps)


def modulate(field, shift, scale):
    return layer_norm(field) * (1.0 + scale) + shift


def head_norm(field, gain):
    height, width = field.shape
    shaped = field.reshape(height, width // HDIM, HDIM)
    power = jnp.mean(shaped * shaped, axis=-1, keepdims=True)
    return (shaped * lax.rsqrt(power + eps) * gain).reshape(height, width)


def attend(carry, queries, piece, valid):
    highest, total, mixed = carry
    height, width = queries.shape
    heads = width // HDIM
    keys = piece[:, :width].reshape(-1, heads, HDIM)
    values = piece[:, width:].reshape(-1, heads, HDIM)
    scores = jnp.einsum(
        "qhd,khd->qhk",
        queries.reshape(height, heads, HDIM),
        keys,
        preferred_element_type=jnp.float32,
    ) * HDIM ** (-0.5)
    scores = jnp.where(valid[None, None, :], scores, masked_score)
    new_high = jnp.maximum(highest, jnp.max(scores, axis=-1))
    expo = jnp.where(valid[None, None, :], jnp.exp(scores - new_high[..., None]), 0.0)
    keep = jnp.exp(highest - new_high)
    total = total * keep + jnp.sum(expo, axis=-1)
    mixed = mixed * keep[..., None] + jnp.einsum(
        "qhk,khd->qhd", expo.astype(jnp.bfloat16), values, preferred_element_type=jnp.float32
    )
    return (new_high, total, mixed)


def empty_carry(height, heads):
    return (
        jnp.full((height, heads), masked_score, jnp.float32),
        jnp.zeros((height, heads), jnp.float32),
        jnp.zeros((height, heads, HDIM), jnp.float32),
    )


def shards(
    image_in,
    text_in,
    text_length,
    entry_order,
    step_index,
    image_modulation,
    text_modulation,
    image_to_heads,
    text_to_heads,
    head_gain,
    image_from_heads,
    text_from_heads,
    image_up,
    image_down,
    stale_cache,
    final_modulation,
    final_weight,
    latents,
):
    section = lax.axis_index("section")
    last_section = lax.axis_size("section") - 1
    position = lax.axis_index("tok")
    image_x = image_in[0, 0].astype(jnp.float32)
    text_x = text_in[0, 0].astype(jnp.float32)
    image_rows = image_x.shape[0]
    width = image_x.shape[1]
    heads = width // HDIM
    patch = lax.dynamic_index_in_dim(entry_order[0], section, 0, False)
    step_now = lax.dynamic_index_in_dim(step_index[0], patch, 0, False)
    modul = (
        lax.dynamic_index_in_dim(image_modulation[0], step_now, 0, False)
        .astype(jnp.float32)
        .reshape(6, width)
    )
    text_mod = (
        lax.dynamic_index_in_dim(text_modulation[0], step_now, 0, False)
        .astype(jnp.float32)
        .reshape(3, width)
    )
    image_normed = modulate(image_x, modul[0], modul[1]).astype(jnp.bfloat16)
    text_normed = modulate(text_x, text_mod[0], text_mod[1]).astype(jnp.bfloat16)
    every_image, every_text = (
        lax.all_gather(image_normed, "tok", axis=0, tiled=True),
        lax.all_gather(text_normed, "tok", axis=0, tiled=True),
    )
    image_cols = jnp.dot(every_image, image_to_heads[0], preferred_element_type=jnp.float32).astype(
        jnp.bfloat16
    )
    text_cols = jnp.dot(every_text, text_to_heads[0], preferred_element_type=jnp.float32).astype(
        jnp.bfloat16
    )
    image_proj, text_proj = (
        lax.all_to_all(image_cols, "tok", split_axis=0, concat_axis=1, tiled=True),
        lax.all_to_all(text_cols, "tok", split_axis=0, concat_axis=1, tiled=True),
    )
    gains = head_gain[0]
    image_query = head_norm(image_proj[:, :width].astype(jnp.float32), gains[0]).astype(
        jnp.bfloat16
    )
    image_key = head_norm(image_proj[:, width : 2 * width].astype(jnp.float32), gains[1]).astype(
        jnp.bfloat16
    )
    text_query = head_norm(text_proj[:, :width].astype(jnp.float32), gains[2]).astype(jnp.bfloat16)
    text_key = head_norm(text_proj[:, width : 2 * width].astype(jnp.float32), gains[3]).astype(
        jnp.bfloat16
    )
    fresh_image = jnp.concatenate([image_key, image_proj[:, 2 * width :]], axis=1)
    fresh_text = jnp.concatenate([text_key, text_proj[:, 2 * width :]], axis=1)
    queries = jnp.concatenate([image_query, text_query], axis=0)
    query_rows = queries.shape[0]
    patch_rows = lax.all_gather(fresh_image, "tok", axis=0, tiled=True)
    stale = stale_cache[0, 0]
    cache_rows = stale.shape[0]
    patch_len = patch_rows.shape[0]
    first_row = position * cache_rows
    begin = patch * patch_len
    offset = jnp.clip(first_row - begin, 0, patch_len - cache_rows)
    window = lax.dynamic_slice_in_dim(patch_rows, offset, cache_rows, 0)
    inside = jnp.logical_and(first_row >= begin, first_row < begin + patch_len)
    current = jnp.where(inside, window, stale)
    text_count = text_length[0]
    piece = lax.all_gather(current, "tok", axis=0, tiled=True)
    carry = attend(
        empty_carry(query_rows, heads), queries, piece, jnp.ones((piece.shape[0],), bool)
    )
    piece = lax.all_gather(fresh_text, "tok", axis=0, tiled=True)
    where_text = jnp.arange(piece.shape[0], dtype=jnp.int32)
    highest, total, mixed = attend(carry, queries, piece, where_text < text_count)
    attended = (mixed / total[..., None]).reshape(query_rows, width).astype(jnp.bfloat16)
    every_image_att, every_text_att = (
        lax.all_gather(attended[:image_rows], "tok", axis=0, tiled=True),
        lax.all_gather(attended[image_rows:], "tok", axis=0, tiled=True),
    )
    image_back_cols = jnp.dot(
        every_image_att, image_from_heads[0], preferred_element_type=jnp.float32
    ).astype(jnp.bfloat16)
    text_back_cols = jnp.dot(
        every_text_att, text_from_heads[0], preferred_element_type=jnp.float32
    ).astype(jnp.bfloat16)
    image_back, text_back = (
        lax.all_to_all(image_back_cols, "tok", split_axis=0, concat_axis=1, tiled=True),
        lax.all_to_all(text_back_cols, "tok", split_axis=0, concat_axis=1, tiled=True),
    )
    image_mid = image_x + modul[2] * image_back.astype(jnp.float32)
    text_out = (text_x + text_mod[2] * text_back.astype(jnp.float32)).astype(jnp.bfloat16)
    mlp_normed = modulate(image_mid, modul[3], modul[4]).astype(jnp.bfloat16)
    up_weight = image_up[0]
    down_weight = image_down[0]
    hidden = jax.nn.gelu(
        jnp.dot(
            lax.all_gather(mlp_normed, "tok", axis=0, tiled=True),
            up_weight,
            preferred_element_type=jnp.float32,
        ),
        approximate=True,
    ).astype(jnp.bfloat16)
    reduced = lax.psum_scatter(
        jnp.dot(hidden, down_weight, preferred_element_type=jnp.float32),
        "tok",
        scatter_dimension=0,
        tiled=True,
    )
    image_out = (image_mid + modul[5] * reduced).astype(jnp.bfloat16)
    joined = from_behind(jnp.concatenate([image_out, text_out], axis=0), "section", 1)
    image_next = joined[:image_rows]
    text_next = joined[image_rows:]
    final_source = jnp.where(section == last_section, image_out, image_next)
    patch_last = entry_order[0, last_section]
    step_last = lax.dynamic_index_in_dim(step_index[0], patch_last, 0, False)
    final_mod = (
        lax.dynamic_index_in_dim(final_modulation, step_last, 0, False)
        .astype(jnp.float32)
        .reshape(2, width)
    )
    normed = modulate(final_source.astype(jnp.float32), final_mod[0], final_mod[1]).astype(
        jnp.bfloat16
    )
    velocity = jnp.dot(normed, final_weight, preferred_element_type=jnp.float32)
    latents_next = latents[0] + -1.0 / TSTEPS * velocity
    return (image_next[None, None], text_next[None, None], current[None, None], latents_next[None])


def unit_rms(block, gain):
    power = jnp.mean(block * block, axis=-1, keepdims=True)
    return (block * lax.rsqrt(power + eps) * gain).astype(jnp.bfloat16)


def head_kernel(
    patch_ref, count_ref, q_ref, k_ref, v_ref, ks_ref, vs_ref, gain_ref, out_ref, keys, values
):
    cache_rows = ks_ref.shape[0]
    rows = k_ref.shape[0]
    image_rows = rows - (keys.shape[0] - cache_rows)
    text_rows = rows - image_rows
    gains = gain_ref[...]
    f32 = jnp.float32
    begin = pl.multiple_of(patch_ref[0] * image_rows, image_rows)
    keys[pl.ds(0, cache_rows), :] = ks_ref[...]
    values[pl.ds(0, cache_rows), :] = vs_ref[...]
    keys[pl.ds(begin, image_rows), :] = unit_rms(k_ref[pl.ds(0, image_rows), :].astype(f32), gains[1:2])
    values[pl.ds(begin, image_rows), :] = v_ref[pl.ds(0, image_rows), :]
    keys[pl.ds(cache_rows, text_rows), :] = unit_rms(
        k_ref[pl.ds(image_rows, text_rows), :].astype(f32), gains[3:4]
    )
    values[pl.ds(cache_rows, text_rows), :] = v_ref[pl.ds(image_rows, text_rows), :]
    all_keys = keys[...]
    all_values = values[...]
    column = lax.broadcasted_iota(jnp.int32, (1, cache_rows + text_rows), 1)
    valid = column < cache_rows + count_ref[0]
    chunk = image_rows
    for part in range(rows // chunk):
        span = pl.ds(part * chunk, chunk)
        gain = gains[0:1] if part == 0 else gains[2:3]
        query = unit_rms(q_ref[span, :].astype(f32), gain)
        scores = lax.dot_general(
            query, all_keys, (((1,), (1,)), ((), ())), preferred_element_type=f32
        ) * HDIM ** (-0.5)
        scores = jnp.where(valid, scores, masked_score)
        highest = jnp.max(scores, axis=-1, keepdims=True)
        expo = jnp.exp(scores - highest)
        total = jnp.sum(expo, axis=-1, keepdims=True)
        mixed = jnp.dot(expo.astype(jnp.bfloat16), all_values, preferred_element_type=f32)
        out_ref[span, :] = (mixed / total).astype(jnp.bfloat16)


def head_attention(patch, count, q, k, v, stale_k, stale_v, gains):
    rows, width = q.shape
    cache_rows = stale_k.shape[0]
    image_rows = patch_rows_of(cache_rows)
    total_keys = cache_rows + rows - image_rows
    tall = pl.BlockSpec((rows, HDIM), lambda h, *_: (0, h))
    kept = pl.BlockSpec((cache_rows, HDIM), lambda h, *_: (0, h))
    return pl.pallas_call(
        head_kernel,
        out_shape=jax.ShapeDtypeStruct((rows, width), jnp.bfloat16),
        grid_spec=pltpu.PrefetchScalarGridSpec(
            num_scalar_prefetch=2,
            grid=(width // HDIM,),
            in_specs=[
                tall,
                tall,
                tall,
                kept,
                kept,
                pl.BlockSpec((4, HDIM), lambda h, *_: (0, 0)),
            ],
            out_specs=tall,
            scratch_shapes=[
                pltpu.VMEM((total_keys, HDIM), jnp.bfloat16),
                pltpu.VMEM((total_keys, HDIM), jnp.bfloat16),
            ],
        ),
        compiler_params=pltpu.CompilerParams(vmem_limit_bytes=32 * 1024 * 1024),
        cost_estimate=pl.CostEstimate(
            flops=4 * rows * total_keys * width,
            bytes_accessed=2 * width * (4 * rows + 2 * cache_rows),
            transcendentals=rows * total_keys * (width // HDIM),
        ),
    )(patch[None], count[None], q, k, v, stale_k, stale_v, gains)


def patch_rows_of(cache_rows):
    return cache_rows // PATCHES


def swap_heads(cols, position):
    count = lax.axis_size("tok")
    block = cols.shape[1] // 3
    first, second, third = (cols[:, i * block : (i + 1) * block] for i in range(3))
    even = position % 2 == 0
    near = lax.ppermute(second, "tok", [(0, 1), (1, 0), (2, 3), (3, 2)])
    far = lax.ppermute(
        jnp.where(even, third, first), "tok", [(0, 2), (2, 0), (1, 3), (3, 1)]
    )
    stay = jnp.where(even, first, third)
    query = jnp.where(position == 0, stay, jnp.where(position == 1, near, far))
    key = jnp.where((position == 0) | (position == 3), near, stay)
    value = jnp.where(position == 3, stay, jnp.where(position == 2, near, far))
    return query, key, value


def shards_by_head(
    image_in,
    text_in,
    text_length,
    entry_order,
    step_index,
    image_modulation,
    text_modulation,
    image_to_heads,
    text_to_heads,
    head_gain,
    image_from_heads,
    text_from_heads,
    image_up,
    image_down,
    stale_cache,
    final_modulation,
    final_weight,
    latents,
):
    f32, bf16 = jnp.float32, jnp.bfloat16
    section = lax.axis_index("section")
    last_section = lax.axis_size("section") - 1
    position = lax.axis_index("tok")
    count = lax.axis_size("tok")
    text_x = text_in[0, 0].astype(f32)
    image_rows, width = image_in.shape[2:]
    text_rows = text_in.shape[2]
    patch_len = image_rows * count
    share = width // count
    patch = lax.dynamic_index_in_dim(entry_order[0], section, 0, False)
    step_now = lax.dynamic_index_in_dim(step_index[0], patch, 0, False)
    modul = (
        lax.dynamic_index_in_dim(image_modulation[0], step_now, 0, False)
        .astype(f32)
        .reshape(6, width)
    )
    text_mod = (
        lax.dynamic_index_in_dim(text_modulation[0], step_now, 0, False)
        .astype(f32)
        .reshape(3, width)
    )
    stale = stale_cache[0, 0]
    cache_rows = stale.shape[0]
    text_normed = modulate(text_x, text_mod[0], text_mod[1]).astype(bf16)
    own = jnp.concatenate([image_in[0, 0], text_normed], axis=0)
    every = lax.all_gather(own, "tok", axis=0, tiled=False)
    every, late_stale = lax.optimization_barrier((every, stale))
    stale_heads = lax.all_to_all(
        late_stale.reshape(cache_rows, 2, count, share), "tok", split_axis=2, concat_axis=0, tiled=False
    )
    stale_k = stale_heads[:, :, 0].reshape(count * cache_rows, share)
    stale_v = stale_heads[:, :, 1].reshape(count * cache_rows, share)
    every_image_x = every[:, :image_rows].reshape(patch_len, width).astype(f32)
    every_text = every[:, image_rows:].reshape(count * text_rows, width)
    every_image = modulate(every_image_x, modul[0], modul[1]).astype(bf16)
    image_cols = jnp.dot(every_image, image_to_heads[0], preferred_element_type=f32).astype(bf16)
    text_cols = jnp.dot(every_text, text_to_heads[0], preferred_element_type=f32).astype(bf16)
    query, key, value = swap_heads(jnp.concatenate([image_cols, text_cols], axis=0), position)
    gains = head_gain[0]
    image_key = head_norm(key[:patch_len].astype(f32), gains[1]).astype(bf16)
    attended = head_attention(patch, text_length[0], query, key, value, stale_k, stale_v, gains)
    fresh = lax.all_gather(
        jnp.stack([image_key, value[:patch_len]], axis=0), "tok", axis=0, tiled=False
    )
    patch_rows = fresh.transpose(2, 1, 0, 3).reshape(patch_len, 2 * width)
    first_row = position * cache_rows
    begin = patch * patch_len
    offset = jnp.clip(first_row - begin, 0, patch_len - cache_rows)
    window = lax.dynamic_slice_in_dim(patch_rows, offset, cache_rows, 0)
    inside = jnp.logical_and(first_row >= begin, first_row < begin + patch_len)
    current = jnp.where(inside, window, stale)
    image_att = lax.all_gather(attended[:patch_len], "tok", axis=1, tiled=True)
    image_att, text_own = lax.optimization_barrier((image_att, attended[patch_len:]))
    text_att = lax.all_gather(text_own, "tok", axis=0, tiled=False)
    image_back_cols = jnp.dot(image_att, image_from_heads[0], preferred_element_type=f32).astype(bf16)
    image_back = lax.all_gather(image_back_cols, "tok", axis=1, tiled=True)
    text_back_cols = jnp.einsum(
        "trd,tdc->rc",
        text_att,
        text_from_heads[0].reshape(count, share, share),
        preferred_element_type=f32,
    ).astype(bf16)
    text_back = lax.all_to_all(text_back_cols, "tok", split_axis=0, concat_axis=1, tiled=True)
    image_mid = every_image_x + modul[2] * image_back.astype(f32)
    text_out = (text_x + text_mod[2] * text_back.astype(f32)).astype(bf16)
    text_next = from_behind(text_out, "section", 1)
    mlp_normed = modulate(image_mid, modul[3], modul[4]).astype(bf16)
    hidden = jax.nn.gelu(
        jnp.dot(mlp_normed, image_up[0], preferred_element_type=f32), approximate=True
    ).astype(bf16)
    partial = jnp.dot(hidden, image_down[0], preferred_element_type=f32)
    parts = lax.all_to_all(
        partial.astype(bf16).reshape(count, image_rows, width),
        "tok",
        split_axis=0,
        concat_axis=0,
        tiled=False,
    )
    reduced = jnp.sum(parts.astype(f32), axis=0)
    mid_own = lax.dynamic_slice_in_dim(image_mid, position * image_rows, image_rows, 0)
    image_out = (mid_own + modul[5] * reduced).astype(bf16)
    image_next = from_behind(image_out, "section", 1)
    final_source = jnp.where(section == last_section, image_out, image_next)
    patch_last = entry_order[0, last_section]
    step_last = lax.dynamic_index_in_dim(step_index[0], patch_last, 0, False)
    final_mod = (
        lax.dynamic_index_in_dim(final_modulation, step_last, 0, False)
        .astype(f32)
        .reshape(2, width)
    )
    normed = modulate(final_source.astype(f32), final_mod[0], final_mod[1]).astype(bf16)
    velocity = jnp.dot(normed, final_weight, preferred_element_type=f32)
    latents_next = latents[0] + -1.0 / TSTEPS * velocity
    return (image_next[None, None], text_next[None, None], current[None, None], latents_next[None])


def solution(mesh):
    placed = (
        P("section", "grp", "tok", None),
        P("section", "grp", "tok", None),
        P("grp"),
        P("grp", None),
        P("grp", None),
        P("section", None, None),
        P("section", None, None),
        P("section", None, "tok"),
        P("section", None, "tok"),
        P("section", None, None),
        P("section", None, "tok"),
        P("section", None, "tok"),
        P("section", None, "tok"),
        P("section", "tok", None),
        P("section", "grp", "tok", None),
        P(),
        P(None, "section"),
        P("grp", "tok", "section"),
    )
    return jax.shard_map(
        shards_by_head if mesh.shape["tok"] == 4 else shards,
        mesh=mesh,
        in_specs=placed,
        out_specs=(
            P("section", "grp", "tok", None),
            P("section", "grp", "tok", None),
            P("section", "grp", "tok", None),
            P("grp", "tok", "section"),
        ),
        check_vma=False,
    )
```

```python
import jax
import jax.numpy as jnp
from jax import lax
from jax.experimental import pallas as pl
from jax.experimental.pallas import tpu as pltpu
from jax.sharding import PartitionSpec as P

HDIM = 128
TSTEPS = 4
PATCHES = 4


eps = 1e-06
masked_score = -1e30


def from_behind(block, axis, distance):
    devices = range(lax.axis_size(axis))
    route = [((i - distance) % len(devices), i) for i in devices]
    return lax.ppermute(block, axis, route)


def layer_norm(field):
    mean = jnp.mean(field, axis=-1, keepdims=True)
    centred = field - mean
    spread = jnp.mean(centred * centred, axis=-1, keepdims=True)
    return centred * lax.rsqrt(spread + eps)


def modulate(field, shift, scale):
    return layer_norm(field) * (1.0 + scale) + shift


def head_norm(field, gain):
    height, width = field.shape
    shaped = field.reshape(height, width // HDIM, HDIM)
    power = jnp.mean(shaped * shaped, axis=-1, keepdims=True)
    return (shaped * lax.rsqrt(power + eps) * gain).reshape(height, width)


def attend(carry, queries, piece, valid):
    highest, total, mixed = carry
    height, width = queries.shape
    heads = width // HDIM
    keys = piece[:, :width].reshape(-1, heads, HDIM)
    values = piece[:, width:].reshape(-1, heads, HDIM)
    scores = jnp.einsum(
        "qhd,khd->qhk",
        queries.reshape(height, heads, HDIM),
        keys,
        preferred_element_type=jnp.float32,
    ) * HDIM ** (-0.5)
    scores = jnp.where(valid[None, None, :], scores, masked_score)
    new_high = jnp.maximum(highest, jnp.max(scores, axis=-1))
    expo = jnp.where(valid[None, None, :], jnp.exp(scores - new_high[..., None]), 0.0)
    keep = jnp.exp(highest - new_high)
    total = total * keep + jnp.sum(expo, axis=-1)
    mixed = mixed * keep[..., None] + jnp.einsum(
        "qhk,khd->qhd", expo.astype(jnp.bfloat16), values, preferred_element_type=jnp.float32
    )
    return (new_high, total, mixed)


def empty_carry(height, heads):
    return (
        jnp.full((height, heads), masked_score, jnp.float32),
        jnp.zeros((height, heads), jnp.float32),
        jnp.zeros((height, heads, HDIM), jnp.float32),
    )


def shards(
    image_in,
    text_in,
    text_length,
    entry_order,
    step_index,
    image_modulation,
    text_modulation,
    image_to_heads,
    text_to_heads,
    head_gain,
    image_from_heads,
    text_from_heads,
    image_up,
    image_down,
    stale_cache,
    final_modulation,
    final_weight,
    latents,
):
    section = lax.axis_index("section")
    last_section = lax.axis_size("section") - 1
    position = lax.axis_index("tok")
    image_x = image_in[0, 0].astype(jnp.float32)
    text_x = text_in[0, 0].astype(jnp.float32)
    image_rows = image_x.shape[0]
    width = image_x.shape[1]
    heads = width // HDIM
    patch = lax.dynamic_index_in_dim(entry_order[0], section, 0, False)
    step_now = lax.dynamic_index_in_dim(step_index[0], patch, 0, False)
    modul = (
        lax.dynamic_index_in_dim(image_modulation[0], step_now, 0, False)
        .astype(jnp.float32)
        .reshape(6, width)
    )
    text_mod = (
        lax.dynamic_index_in_dim(text_modulation[0], step_now, 0, False)
        .astype(jnp.float32)
        .reshape(3, width)
    )
    image_normed = modulate(image_x, modul[0], modul[1]).astype(jnp.bfloat16)
    text_normed = modulate(text_x, text_mod[0], text_mod[1]).astype(jnp.bfloat16)
    every_image, every_text = (
        lax.all_gather(image_normed, "tok", axis=0, tiled=True),
        lax.all_gather(text_normed, "tok", axis=0, tiled=True),
    )
    image_cols = jnp.dot(every_image, image_to_heads[0], preferred_element_type=jnp.float32).astype(
        jnp.bfloat16
    )
    text_cols = jnp.dot(every_text, text_to_heads[0], preferred_element_type=jnp.float32).astype(
        jnp.bfloat16
    )
    image_proj, text_proj = (
        lax.all_to_all(image_cols, "tok", split_axis=0, concat_axis=1, tiled=True),
        lax.all_to_all(text_cols, "tok", split_axis=0, concat_axis=1, tiled=True),
    )
    gains = head_gain[0]
    image_query = head_norm(image_proj[:, :width].astype(jnp.float32), gains[0]).astype(
        jnp.bfloat16
    )
    image_key = head_norm(image_proj[:, width : 2 * width].astype(jnp.float32), gains[1]).astype(
        jnp.bfloat16
    )
    text_query = head_norm(text_proj[:, :width].astype(jnp.float32), gains[2]).astype(jnp.bfloat16)
    text_key = head_norm(text_proj[:, width : 2 * width].astype(jnp.float32), gains[3]).astype(
        jnp.bfloat16
    )
    fresh_image = jnp.concatenate([image_key, image_proj[:, 2 * width :]], axis=1)
    fresh_text = jnp.concatenate([text_key, text_proj[:, 2 * width :]], axis=1)
    queries = jnp.concatenate([image_query, text_query], axis=0)
    query_rows = queries.shape[0]
    patch_rows = lax.all_gather(fresh_image, "tok", axis=0, tiled=True)
    stale = stale_cache[0, 0]
    cache_rows = stale.shape[0]
    patch_len = patch_rows.shape[0]
    first_row = position * cache_rows
    begin = patch * patch_len
    offset = jnp.clip(first_row - begin, 0, patch_len - cache_rows)
    window = lax.dynamic_slice_in_dim(patch_rows, offset, cache_rows, 0)
    inside = jnp.logical_and(first_row >= begin, first_row < begin + patch_len)
    current = jnp.where(inside, window, stale)
    text_count = text_length[0]
    piece = lax.all_gather(current, "tok", axis=0, tiled=True)
    carry = attend(
        empty_carry(query_rows, heads), queries, piece, jnp.ones((piece.shape[0],), bool)
    )
    piece = lax.all_gather(fresh_text, "tok", axis=0, tiled=True)
    where_text = jnp.arange(piece.shape[0], dtype=jnp.int32)
    highest, total, mixed = attend(carry, queries, piece, where_text < text_count)
    attended = (mixed / total[..., None]).reshape(query_rows, width).astype(jnp.bfloat16)
    every_image_att, every_text_att = (
        lax.all_gather(attended[:image_rows], "tok", axis=0, tiled=True),
        lax.all_gather(attended[image_rows:], "tok", axis=0, tiled=True),
    )
    image_back_cols = jnp.dot(
        every_image_att, image_from_heads[0], preferred_element_type=jnp.float32
    ).astype(jnp.bfloat16)
    text_back_cols = jnp.dot(
        every_text_att, text_from_heads[0], preferred_element_type=jnp.float32
    ).astype(jnp.bfloat16)
    image_back, text_back = (
        lax.all_to_all(image_back_cols, "tok", split_axis=0, concat_axis=1, tiled=True),
        lax.all_to_all(text_back_cols, "tok", split_axis=0, concat_axis=1, tiled=True),
    )
    image_mid = image_x + modul[2] * image_back.astype(jnp.float32)
    text_out = (text_x + text_mod[2] * text_back.astype(jnp.float32)).astype(jnp.bfloat16)
    mlp_normed = modulate(image_mid, modul[3], modul[4]).astype(jnp.bfloat16)
    up_weight = image_up[0]
    down_weight = image_down[0]
    hidden = jax.nn.gelu(
        jnp.dot(
            lax.all_gather(mlp_normed, "tok", axis=0, tiled=True),
            up_weight,
            preferred_element_type=jnp.float32,
        ),
        approximate=True,
    ).astype(jnp.bfloat16)
    reduced = lax.psum_scatter(
        jnp.dot(hidden, down_weight, preferred_element_type=jnp.float32),
        "tok",
        scatter_dimension=0,
        tiled=True,
    )
    image_out = (image_mid + modul[5] * reduced).astype(jnp.bfloat16)
    joined = from_behind(jnp.concatenate([image_out, text_out], axis=0), "section", 1)
    image_next = joined[:image_rows]
    text_next = joined[image_rows:]
    final_source = jnp.where(section == last_section, image_out, image_next)
    patch_last = entry_order[0, last_section]
    step_last = lax.dynamic_index_in_dim(step_index[0], patch_last, 0, False)
    final_mod = (
        lax.dynamic_index_in_dim(final_modulation, step_last, 0, False)
        .astype(jnp.float32)
        .reshape(2, width)
    )
    normed = modulate(final_source.astype(jnp.float32), final_mod[0], final_mod[1]).astype(
        jnp.bfloat16
    )
    velocity = jnp.dot(normed, final_weight, preferred_element_type=jnp.float32)
    latents_next = latents[0] + -1.0 / TSTEPS * velocity
    return (image_next[None, None], text_next[None, None], current[None, None], latents_next[None])


def unit_rms(block, gain):
    power = jnp.mean(block * block, axis=-1, keepdims=True)
    return (block * lax.rsqrt(power + eps) * gain).astype(jnp.bfloat16)


def head_kernel(
    patch_ref, count_ref, q_ref, k_ref, v_ref, ks_ref, vs_ref, gain_ref, out_ref, keys, values
):
    cache_rows = ks_ref.shape[0]
    rows = k_ref.shape[0]
    image_rows = rows - (keys.shape[0] - cache_rows)
    text_rows = rows - image_rows
    gains = gain_ref[...]
    f32 = jnp.float32
    begin = pl.multiple_of(patch_ref[0] * image_rows, image_rows)
    keys[pl.ds(0, cache_rows), :] = ks_ref[...]
    values[pl.ds(0, cache_rows), :] = vs_ref[...]
    keys[pl.ds(begin, image_rows), :] = unit_rms(k_ref[pl.ds(0, image_rows), :].astype(f32), gains[1:2])
    values[pl.ds(begin, image_rows), :] = v_ref[pl.ds(0, image_rows), :]
    keys[pl.ds(cache_rows, text_rows), :] = unit_rms(
        k_ref[pl.ds(image_rows, text_rows), :].astype(f32), gains[3:4]
    )
    values[pl.ds(cache_rows, text_rows), :] = v_ref[pl.ds(image_rows, text_rows), :]
    all_keys = keys[...]
    all_values = values[...]
    column = lax.broadcasted_iota(jnp.int32, (1, cache_rows + text_rows), 1)
    valid = column < cache_rows + count_ref[0]
    chunk = image_rows
    for part in range(rows // chunk):
        span = pl.ds(part * chunk, chunk)
        gain = gains[0:1] if part == 0 else gains[2:3]
        query = unit_rms(q_ref[span, :].astype(f32), gain)
        scores = lax.dot_general(
            query, all_keys, (((1,), (1,)), ((), ())), preferred_element_type=f32
        ) * HDIM ** (-0.5)
        scores = jnp.where(valid, scores, masked_score)
        highest = jnp.max(scores, axis=-1, keepdims=True)
        expo = jnp.exp(scores - highest)
        total = jnp.sum(expo, axis=-1, keepdims=True)
        mixed = jnp.dot(expo.astype(jnp.bfloat16), all_values, preferred_element_type=f32)
        out_ref[span, :] = (mixed / total).astype(jnp.bfloat16)


def head_attention(patch, count, q, k, v, stale_k, stale_v, gains):
    rows, width = q.shape
    cache_rows = stale_k.shape[0]
    image_rows = patch_rows_of(cache_rows)
    total_keys = cache_rows + rows - image_rows
    tall = pl.BlockSpec((rows, HDIM), lambda h, *_: (0, h))
    kept = pl.BlockSpec((cache_rows, HDIM), lambda h, *_: (0, h))
    return pl.pallas_call(
        head_kernel,
        out_shape=jax.ShapeDtypeStruct((rows, width), jnp.bfloat16),
        grid_spec=pltpu.PrefetchScalarGridSpec(
            num_scalar_prefetch=2,
            grid=(width // HDIM,),
            in_specs=[
                tall,
                tall,
                tall,
                kept,
                kept,
                pl.BlockSpec((4, HDIM), lambda h, *_: (0, 0)),
            ],
            out_specs=tall,
            scratch_shapes=[
                pltpu.VMEM((total_keys, HDIM), jnp.bfloat16),
                pltpu.VMEM((total_keys, HDIM), jnp.bfloat16),
            ],
        ),
        compiler_params=pltpu.CompilerParams(vmem_limit_bytes=32 * 1024 * 1024),
        cost_estimate=pl.CostEstimate(
            flops=4 * rows * total_keys * width,
            bytes_accessed=2 * width * (4 * rows + 2 * cache_rows),
            transcendentals=rows * total_keys * (width // HDIM),
        ),
    )(patch[None], count[None], q, k, v, stale_k, stale_v, gains)


def patch_rows_of(cache_rows):
    return cache_rows // PATCHES


def swap_heads(cols, position):
    count = lax.axis_size("tok")
    block = cols.shape[1] // 3
    first, second, third = (cols[:, i * block : (i + 1) * block] for i in range(3))
    even = position % 2 == 0
    near = lax.ppermute(second, "tok", [(0, 1), (1, 0), (2, 3), (3, 2)])
    far = lax.ppermute(
        jnp.where(even, third, first), "tok", [(0, 2), (2, 0), (1, 3), (3, 1)]
    )
    stay = jnp.where(even, first, third)
    query = jnp.where(position == 0, stay, jnp.where(position == 1, near, far))
    key = jnp.where((position == 0) | (position == 3), near, stay)
    value = jnp.where(position == 3, stay, jnp.where(position == 2, near, far))
    return query, key, value


def shards_by_head(
    image_in,
    text_in,
    text_length,
    entry_order,
    step_index,
    image_modulation,
    text_modulation,
    image_to_heads,
    text_to_heads,
    head_gain,
    image_from_heads,
    text_from_heads,
    image_up,
    image_down,
    stale_cache,
    final_modulation,
    final_weight,
    latents,
):
    f32, bf16 = jnp.float32, jnp.bfloat16
    section = lax.axis_index("section")
    last_section = lax.axis_size("section") - 1
    position = lax.axis_index("tok")
    count = lax.axis_size("tok")
    text_x = text_in[0, 0].astype(f32)
    image_rows, width = image_in.shape[2:]
    text_rows = text_in.shape[2]
    patch_len = image_rows * count
    share = width // count
    patch = lax.dynamic_index_in_dim(entry_order[0], section, 0, False)
    step_now = lax.dynamic_index_in_dim(step_index[0], patch, 0, False)
    modul = (
        lax.dynamic_index_in_dim(image_modulation[0], step_now, 0, False)
        .astype(f32)
        .reshape(6, width)
    )
    text_mod = (
        lax.dynamic_index_in_dim(text_modulation[0], step_now, 0, False)
        .astype(f32)
        .reshape(3, width)
    )
    stale = stale_cache[0, 0]
    cache_rows = stale.shape[0]
    stale_heads = lax.all_to_all(
        stale.reshape(cache_rows, 2, count, share), "tok", split_axis=2, concat_axis=0, tiled=False
    )
    stale_k = stale_heads[:, :, 0].reshape(count * cache_rows, share)
    stale_v = stale_heads[:, :, 1].reshape(count * cache_rows, share)
    text_normed = modulate(text_x, text_mod[0], text_mod[1]).astype(bf16)
    own = jnp.concatenate([image_in[0, 0], text_normed], axis=0)
    every = lax.all_gather(own, "tok", axis=0, tiled=False)
    every_image_x = every[:, :image_rows].reshape(patch_len, width).astype(f32)
    every_text = every[:, image_rows:].reshape(count * text_rows, width)
    every_image = modulate(every_image_x, modul[0], modul[1]).astype(bf16)
    image_cols = jnp.dot(every_image, image_to_heads[0], preferred_element_type=f32).astype(bf16)
    text_cols = jnp.dot(every_text, text_to_heads[0], preferred_element_type=f32).astype(bf16)
    query, key, value = swap_heads(jnp.concatenate([image_cols, text_cols], axis=0), position)
    gains = head_gain[0]
    image_key = head_norm(key[:patch_len].astype(f32), gains[1]).astype(bf16)
    attended = head_attention(patch, text_length[0], query, key, value, stale_k, stale_v, gains)
    fresh = lax.all_gather(
        jnp.stack([image_key, value[:patch_len]], axis=0), "tok", axis=0, tiled=False
    )
    patch_rows = fresh.transpose(2, 1, 0, 3).reshape(patch_len, 2 * width)
    first_row = position * cache_rows
    begin = patch * patch_len
    offset = jnp.clip(first_row - begin, 0, patch_len - cache_rows)
    window = lax.dynamic_slice_in_dim(patch_rows, offset, cache_rows, 0)
    inside = jnp.logical_and(first_row >= begin, first_row < begin + patch_len)
    current = jnp.where(inside, window, stale)
    image_att = lax.all_gather(attended[:patch_len], "tok", axis=1, tiled=True)
    image_att, text_own = lax.optimization_barrier((image_att, attended[patch_len:]))
    text_att = lax.all_gather(text_own, "tok", axis=0, tiled=False)
    image_back_cols = jnp.dot(image_att, image_from_heads[0], preferred_element_type=f32).astype(bf16)
    image_back = lax.all_gather(image_back_cols, "tok", axis=1, tiled=True)
    text_back_cols = jnp.einsum(
        "trd,tdc->rc",
        text_att,
        text_from_heads[0].reshape(count, share, share),
        preferred_element_type=f32,
    ).astype(bf16)
    text_back = lax.all_to_all(text_back_cols, "tok", split_axis=0, concat_axis=1, tiled=True)
    image_mid = every_image_x + modul[2] * image_back.astype(f32)
    text_out = (text_x + text_mod[2] * text_back.astype(f32)).astype(bf16)
    text_next = from_behind(text_out, "section", 1)
    mlp_normed = modulate(image_mid, modul[3], modul[4]).astype(bf16)
    hidden = jax.nn.gelu(
        jnp.dot(mlp_normed, image_up[0], preferred_element_type=f32), approximate=True
    ).astype(bf16)
    partial = jnp.dot(hidden, image_down[0], preferred_element_type=f32)
    parts = lax.all_to_all(
        partial.astype(bf16).reshape(count, image_rows, width),
        "tok",
        split_axis=0,
        concat_axis=0,
        tiled=False,
    )
    reduced = jnp.sum(parts.astype(f32), axis=0)
    mid_own = lax.dynamic_slice_in_dim(image_mid, position * image_rows, image_rows, 0)
    image_out = (mid_own + modul[5] * reduced).astype(bf16)
    image_next = from_behind(image_out, "section", 1)
    final_source = jnp.where(section == last_section, image_out, image_next)
    patch_last = entry_order[0, last_section]
    step_last = lax.dynamic_index_in_dim(step_index[0], patch_last, 0, False)
    final_mod = (
        lax.dynamic_index_in_dim(final_modulation, step_last, 0, False)
        .astype(f32)
        .reshape(2, width)
    )
    normed = modulate(final_source.astype(f32), final_mod[0], final_mod[1]).astype(bf16)
    velocity = jnp.dot(normed, final_weight, preferred_element_type=f32)
    latents_next = latents[0] + -1.0 / TSTEPS * velocity
    return (image_next[None, None], text_next[None, None], current[None, None], latents_next[None])


def solution(mesh):
    placed = (
        P("section", "grp", "tok", None),
        P("section", "grp", "tok", None),
        P("grp"),
        P("grp", None),
        P("grp", None),
        P("section", None, None),
        P("section", None, None),
        P("section", None, "tok"),
        P("section", None, "tok"),
        P("section", None, None),
        P("section", None, "tok"),
        P("section", None, "tok"),
        P("section", None, "tok"),
        P("section", "tok", None),
        P("section", "grp", "tok", None),
        P(),
        P(None, "section"),
        P("grp", "tok", "section"),
    )
    return jax.shard_map(
        shards_by_head if mesh.shape["tok"] == 4 else shards,
        mesh=mesh,
        in_specs=placed,
        out_specs=(
            P("section", "grp", "tok", None),
            P("section", "grp", "tok", None),
            P("section", "grp", "tok", None),
            P("grp", "tok", "section"),
        ),
        check_vma=False,
    )
```
